32 devices in a mesh: tm: 8 (over y, x, core), shard: 4 (over z).
Axes of the slice: x: 2, y: 2, z: 4, core: 2. Of those that a mesh axis runs over, the one named last changes fastest.
Arguments:
- frames: bfloat16 [4096, 16384], P('tm', 'shard'), may hold values from -6 to 6
- gain: bfloat16 [256, 16384], P(None, 'shard'), may hold values from -0.0029296875 to 0.0029296875
- transition: float32 [256, 256], replicated, may hold values from -1 to 1
- smoother_gain: float32 [256, 256], replicated, may hold values from -1 to 1
- smoother_map: float32 [256, 256], replicated, may hold values from -9.1552734e-05 to 9.1552734e-05
- emission: bfloat16 [256, 16384], P(None, 'shard'), may hold values from -0.09375 to 0.09375
- noise_precision: float32 [16384], P('shard'), may hold values from 0.5 to 4
Outputs:
- smoothed: float32 [4096, 256], P('tm')
- gradient: float32 [256, 16384], P('tm', 'shard')
The draws below stay inside these ranges and needn't reach their ends.
All inputs are finite; a program needn't handle non-finite values.
Results may differ from the reference program's by a relative error of at most 0.0014.
Values sent between devices are 32-bit elements; how exact they have to be, the bound alone decides.
A program may use at most 128 MiB of HBM per device.

```python
import math
import jax
import jax.numpy as jnp
from jax import lax

LAT = 256
FEAT = 16384
FRAMES = 4096


def damped_rotation(key, shortest, longest):
    key_horizon, key_angle, key_direction = jax.random.split(key, 3)
    pair_count = LAT // 2
    horizon = jnp.exp(jax.random.uniform(key_horizon, (pair_count,), jnp.float32, jnp.log(shortest), jnp.log(longest)))
    radius = jnp.exp(-1.0 / horizon)
    angle = jax.random.uniform(key_angle, (pair_count,), jnp.float32, -jnp.pi, jnp.pi)
    cosine = jnp.repeat(radius * jnp.cos(angle), 2)
    sine = jnp.repeat(radius * jnp.sin(angle), 2)
    row_ids = jnp.arange(LAT)[:, None]
    col_ids = jnp.arange(LAT)[None, :]
    upper = (row_ids % 2 == 0) & (col_ids == row_ids + 1)
    lower = (row_ids % 2 == 1) & (col_ids == row_ids - 1)
    blocks = jnp.where(row_ids == col_ids, cosine[:, None], 0.0)
    blocks = blocks + jnp.where(upper, -sine[:, None], 0.0) + jnp.where(lower, sine[:, None], 0.0)
    direction = jax.random.normal(key_direction, (LAT,), jnp.float32)
    norm_sq = jnp.sum(direction * direction)
    image = jnp.sum(blocks * direction[None, :], axis=1)
    coimage = jnp.sum(blocks * direction[:, None], axis=0)
    quadratic = jnp.sum(direction * image)
    result = blocks - 2.0 / norm_sq * jnp.outer(direction, coimage) - 2.0 / norm_sq * jnp.outer(image, direction)
    return result + 4.0 * quadratic / (norm_sq * norm_sq) * jnp.outer(direction, direction)


def draw_transition(key, part):
    shortest = 30.0
    return damped_rotation(jax.random.fold_in(key, 11), shortest, 4.0 * FRAMES)


def draw_smoother_gain(key, part):
    shortest = 30.0
    return damped_rotation(jax.random.fold_in(key, 23), shortest, 4.0 * FRAMES)


def block_levels(stream_key, shape, pieces, least, high):
    factor_of, own = 1.0, jax.random.fold_in(stream_key, 6)
    for dim, shards_of in pieces:
        draws = jnp.exp(jax.random.uniform(jax.random.fold_in(own, dim), (shards_of,), jnp.float32, least / len(pieces), high / len(pieces)))
        factor_of = factor_of * jnp.repeat(draws, shape[dim] // shards_of).reshape([-1 if axis == dim else 1 for axis in range(len(shape))])
    return factor_of


def centred(stream_key, shape, deviation, most, shards=(), held_as=jnp.bfloat16):
    values = deviation * jax.random.normal(stream_key, shape, jnp.float32)
    if shards:
        values = values * block_levels(stream_key, shape, shards, -0.22, 0.18)
    return jnp.clip(values, -most, most).astype(held_as)


def setup_inputs(seed: int = 0) -> dict:
    splits = jax.random.split(jax.random.key(seed), 8)
    return {
        "frames": centred(splits[0], (FRAMES, FEAT), 1.0, 6.0, ((0, 8), (1, 4))),
        "gain": centred(splits[1], (LAT, FEAT), (FEAT * FRAMES // 16) ** -0.5, 0.0029296875, ((1, 4),)),
        "transition": draw_transition(jax.random.fold_in(splits[7], 71), 0),
        "smoother_gain": draw_smoother_gain(jax.random.fold_in(splits[7], 71), 0),
        "smoother_map": centred(splits[4], (LAT, LAT), (LAT * FRAMES * FRAMES) ** -0.5, 9.1552734375e-05, (), jnp.float32),
        "emission": centred(splits[5], (LAT, FEAT), (LAT * 16) ** -0.5, 0.09375, ((1, 4),)),
        "noise_precision": jnp.clip(jnp.exp(math.log(4.0) - 2.0794415 * jax.random.uniform(splits[6], (FEAT,), jnp.float32) ** block_levels(splits[6], (FEAT,), ((0, 4),), -0.2, 0.2)), 0.5, 4.0),
    }


def reference(frames, gain, transition, smoother_gain, smoother_map, emission, noise_precision):
    drive = jnp.dot(frames, gain.T, preferred_element_type=jnp.float32)

    def filter_step(state_now, drive_row):
        state_next = jnp.dot(transition, state_now, precision=lax.Precision.HIGHEST) + drive_row
        return state_next, state_next

    unused_end, filtered = lax.scan(filter_step, jnp.zeros((LAT,), jnp.float32), drive)
    own_term = jnp.dot(filtered, smoother_map.T, precision=lax.Precision.HIGHEST)
    own_term = own_term.at[-1].set(filtered[-1])

    def smooth_step(state_now, own_row):
        state_next = jnp.dot(smoother_gain, state_now, precision=lax.Precision.HIGHEST) + own_row
        return state_next, state_next

    unused_start, smoothed = lax.scan(smooth_step, jnp.zeros((LAT,), jnp.float32), own_term, reverse=True)
    smoothed_low = smoothed.astype(jnp.bfloat16)
    predicted = jnp.dot(smoothed_low, emission, preferred_element_type=jnp.float32)
    weighted = (noise_precision[None, :] * (frames.astype(jnp.float32) - predicted)).astype(jnp.bfloat16)
    gradient = jnp.dot(smoothed_low.T, weighted, preferred_element_type=jnp.float32) / FRAMES
    return smoothed, gradient
```

```python
import functools

import jax
import jax.numpy as jnp
from jax import lax
from jax.experimental import pallas as pl
from jax.experimental.pallas import tpu as pltpu
from jax.sharding import PartitionSpec as P

MESH = pl.DeviceIdType.MESH
CHUNKS = 4


def bits_of(count):
    return count.bit_length() - 1


def split(value):
    high = value.astype(jnp.bfloat16)
    low = (value - high.astype(jnp.float32)).astype(jnp.bfloat16)
    return high, low


def dot(a, b):
    return jnp.dot(a, b, preferred_element_type=jnp.float32)


def dot3(value, right_high, right_low):
    high, low = split(value)
    return dot(high, right_high) + (dot(low, right_high) + dot(high, right_low))


def row_ids(count):
    return lax.broadcasted_iota(jnp.int32, (count, 1), 0)


def kernel(
    T, S,
    frames, gain, transition, smoother_gain, smoother_map, emission, noise,
    smoothed_out, gradient_out,
    part, landed, state, carry_buf, power, fh, fl, gh, gl, ends_f, ends_s, low, low_t, acc, *rest,
):
    stages = bits_of(T)
    inbox = rest[:stages]
    rs_send, rs_recv, ag_send, ag_recv, ef_send, ef_recv, es_send, es_recv, gr_send, gr_recv = rest[stages:]
    L, features = frames.shape
    lat = gain.shape[0]
    rows = L // S
    levels = bits_of(L)
    mt, ms = lax.axis_index("tm"), lax.axis_index("shard")

    barrier = pltpu.get_barrier_semaphore()

    def greet_s(k, c):
        pl.semaphore_signal(barrier, inc=1, device_id=(mt, lax.rem(ms + k, S)), device_id_type=MESH)
        return c

    def greet_t(k, c):
        pl.semaphore_signal(barrier, inc=1, device_id=(lax.rem(mt + k, T), ms), device_id_type=MESH)
        return c

    lax.fori_loop(1, S, greet_s, 0)
    lax.fori_loop(1, T, greet_t, 0)

    def scatter_copy(k):
        return pltpu.make_async_remote_copy(
            src_ref=part.at[k], dst_ref=landed.at[k], send_sem=rs_send.at[k], recv_sem=rs_recv.at[k],
            device_id=(mt, lax.rem(ms + k, S)), device_id_type=MESH)

    def partial_drive(k):
        owner = lax.rem(ms + k, S)
        block = frames[pl.ds(pl.multiple_of(owner * rows, rows), rows), :]
        part[k] = lax.dot_general(block, gain[...], (((1,), (1,)), ((), ())), preferred_element_type=jnp.float32)

    def drive_step(k, c):
        partial_drive(k)

        @pl.when(k == 1)
        def _():
            pl.semaphore_wait(barrier, S - 1 + T - 1)

        scatter_copy(k).start()
        return c

    lax.fori_loop(1, S, drive_step, 0)
    partial_drive(0)

    power[0] = transition[...].T
    power[1] = smoother_gain[...].T
    fh[0], fl[0] = split(power[0])
    gh[0], gl[0] = split(power[1])

    def square(k, c):
        for i, (h, l) in enumerate(((fh, fl), (gh, gl))):
            value = jnp.dot(power[i], power[i], precision=lax.Precision.HIGHEST, preferred_element_type=jnp.float32)
            power[i] = value
            h[k + 1], l[k + 1] = split(value)
        return c

    lax.fori_loop(0, levels + stages - 1, square, 0)

    total = part[0]
    for k in range(1, S):
        scatter_copy(k).wait_recv()
        total = total + landed[k]
    mine = pl.ds(pl.multiple_of(ms * rows, rows), rows)
    state[mine, :] = total

    def gather_copy(k):
        return pltpu.make_async_remote_copy(
            src_ref=state.at[mine], dst_ref=state.at[mine], send_sem=ag_send.at[k], recv_sem=ag_recv.at[k],
            device_id=(mt, lax.rem(ms + k, S)), device_id_type=MESH)

    def gather_wait(k):
        source = lax.rem(ms + S - k, S)
        there = state.at[pl.ds(pl.multiple_of(source * rows, rows), rows)]
        pltpu.make_async_remote_copy(
            src_ref=there, dst_ref=there, send_sem=ag_send.at[k], recv_sem=ag_recv.at[k],
            device_id=(mt, lax.rem(ms + k, S)), device_id_type=MESH).wait_recv()

    for k in range(1, S):
        gather_copy(k).start()
    map_h, map_l = split(smoother_map[...].T)
    for k in range(1, S):
        gather_wait(k)
    for k in range(1, S):
        gather_copy(k).wait_send()
        scatter_copy(k).wait_send()

    ids = row_ids(L)

    def local_scan(h, l, backward):
        for level in range(levels):
            d = 1 << level
            if d < 8:
                y = dot3(state[...], h[level], l[level])
                if backward:
                    moved = jnp.where(ids < L - d, pltpu.roll(y, L - d, 0), 0.0)
                else:
                    moved = jnp.where(ids >= d, pltpu.roll(y, d, 0), 0.0)
                state[...] = state[...] + moved
            elif backward:
                y = dot3(state[d:, :], h[level], l[level])
                state[: L - d, :] = state[: L - d, :] + y
            else:
                y = dot3(state[: L - d, :], h[level], l[level])
                state[d:, :] = state[d:, :] + y

    def exchange(ends, edge, send, recv):
        ends[mt] = jnp.broadcast_to(edge, (8, lat))

        def copy(k):
            return pltpu.make_async_remote_copy(
                src_ref=ends.at[mt], dst_ref=ends.at[mt], send_sem=send.at[k], recv_sem=recv.at[k],
                device_id=(lax.rem(mt + k, T), ms), device_id_type=MESH)

        def arrive(k):
            source = lax.rem(mt + T - k, T)
            pltpu.make_async_remote_copy(
                src_ref=ends.at[source], dst_ref=ends.at[source], send_sem=send.at[k], recv_sem=recv.at[k],
                device_id=(lax.rem(mt + k, T), ms), device_id_type=MESH).wait_recv()

        for k in range(1, T):
            copy(k).start()
        for k in range(1, T):
            arrive(k)
        for k in range(1, T):
            copy(k).wait_send()
        value = jnp.concatenate([ends[t, 0:1, :] for t in range(T)], axis=0)
        return value

    def arriving(value, h, l, backward):
        small = row_ids(T)
        for level in range(stages):
            d = 1 << level
            y = dot3(value, h[levels + level], l[levels + level])
            if backward:
                y = jnp.where(small < T - d, pltpu.roll(y, T - d, 0), 0.0)
            else:
                y = jnp.where(small >= d, pltpu.roll(y, d, 0), 0.0)
            value = value + y
        pick = mt + 1 if backward else mt - 1
        return jnp.sum(jnp.where(small == pick, value, 0.0), axis=0, keepdims=True)

    def add_carry(carry, h, l, backward):
        small = row_ids(8)
        exponent = 7 - small if backward else small
        value = dot3(jnp.broadcast_to(carry, (8, lat)), h[0], l[0])
        for level in range(3):
            moved = dot3(value, h[level], l[level])
            value = jnp.where((exponent >> level) & 1 == 1, moved, value)
        if backward:
            carry_buf[L - 8 :, :] = value
        else:
            carry_buf[:8, :] = value
        for level in range(3, levels):
            d = 1 << level
            if backward:
                carry_buf[L - 2 * d : L - d, :] = dot3(carry_buf[L - d :, :], h[level], l[level])
            else:
                carry_buf[d : 2 * d, :] = dot3(carry_buf[:d, :], h[level], l[level])
        state[...] = state[...] + carry_buf[...]

    local_scan(fh, fl, False)
    ends = exchange(ends_f, state[L - 1 :, :], ef_send, ef_recv)
    add_carry(arriving(ends, fh, fl, False), fh, fl, False)

    filtered = state[...]
    own = dot3(filtered, map_h, map_l)
    final_row = (ids == L - 1) & (mt == T - 1)
    state[...] = jnp.where(final_row, filtered, own)

    local_scan(gh, gl, True)
    starts = exchange(ends_s, state[:1, :], es_send, es_recv)
    add_carry(arriving(starts, gh, gl, True), gh, gl, True)

    smoothed = state[...]
    smoothed_out[...] = smoothed
    low[...] = smoothed.astype(jnp.bfloat16)
    low_t[...] = smoothed.T.astype(jnp.bfloat16)

    width = features // CHUNKS
    share = lat // T

    def order(c):
        places = list(range(stages))
        return places if c % 2 == 0 else places[:1] + places[:0:-1]

    def bit(place):
        return lax.rem(lax.div(mt, 1 << place), 2)

    def offset(c, stage):
        where = 0
        for earlier in range(stage):
            where = where + bit(order(c)[earlier]) * (T >> (earlier + 1))
        return where

    def halving_copy(c, stage):
        place = order(c)[stage]
        b = bit(place)
        half = T >> (stage + 1)
        partner = mt + (1 - 2 * b) * (1 << place)
        return pltpu.make_async_remote_copy(
            src_ref=acc.at[c, pl.ds(offset(c, stage) + (1 - b) * half, half)],
            dst_ref=inbox[stage].at[c],
            send_sem=gr_send.at[stage, c], recv_sem=gr_recv.at[stage, c],
            device_id=(partner, ms), device_id_type=MESH)

    def compute(c):
        columns = slice(c * width, (c + 1) * width)
        predicted = dot(low[...], emission[:, columns])
        weighted = (noise[:, columns] * (frames[:, columns].astype(jnp.float32) - predicted)).astype(jnp.bfloat16)
        product = dot(low_t[...], weighted)
        for owner in range(T):
            where = 0
            for stage, place in enumerate(order(c)):
                where += (owner >> place & 1) * (T >> (stage + 1))
            acc[c, where] = product[owner * share : (owner + 1) * share, :]

    def take(c, stage):
        halving_copy(c, stage).wait_recv()
        half = T >> (stage + 1)
        keep = pl.ds(offset(c, stage + 1), half)
        acc[c, keep] = acc[c, keep] + inbox[stage][c]

    for step in range(CHUNKS + stages):
        if step < CHUNKS:
            compute(step)
            halving_copy(step, 0).start()
        for stage in range(stages):
            c = step - 1 - stage
            if 0 <= c < CHUNKS:
                take(c, stage)
                if stage + 1 < stages:
                    halving_copy(c, stage + 1).start()
                else:
                    gradient_out[:, c * width : (c + 1) * width] = acc[c, offset(c, stages)] / (L * T)
    for c in range(CHUNKS):
        for stage in range(stages):
            halving_copy(c, stage).wait_send()


def on_device(frames, gain, transition, smoother_gain, smoother_map, emission, noise_precision):
    T, S = lax.axis_size("tm"), lax.axis_size("shard")
    L, features = frames.shape
    lat = gain.shape[0]
    rows = L // S
    stages = bits_of(T)
    levels = bits_of(L) + stages
    width = features // CHUNKS
    f32, b16 = jnp.float32, jnp.bfloat16
    dma = pltpu.SemaphoreType.DMA
    scratch = [
        pltpu.VMEM((S, rows, lat), f32),
        pltpu.VMEM((S, rows, lat), f32),
        pltpu.VMEM((L, lat), f32),
        pltpu.VMEM((L, lat), f32),
        pltpu.VMEM((2, lat, lat), f32),
        pltpu.VMEM((levels, lat, lat), b16),
        pltpu.VMEM((levels, lat, lat), b16),
        pltpu.VMEM((levels, lat, lat), b16),
        pltpu.VMEM((levels, lat, lat), b16),
        pltpu.VMEM((T, 8, lat), f32),
        pltpu.VMEM((T, 8, lat), f32),
        pltpu.VMEM((L, lat), b16),
        pltpu.VMEM((lat, L), b16),
        pltpu.VMEM((CHUNKS, T, lat // T, width), f32),
    ]
    scratch += [pltpu.VMEM((CHUNKS, T >> (s + 1), lat // T, width), f32) for s in range(stages)]
    scratch += [dma((S,))] * 4 + [dma((T,))] * 4 + [dma((stages, CHUNKS))] * 2
    vmem = pl.BlockSpec(memory_space=pltpu.VMEM)
    flops = 6 * L * features * lat
    return pl.pallas_call(
        functools.partial(kernel, T, S),
        out_shape=(
            jax.ShapeDtypeStruct((L, lat), f32),
            jax.ShapeDtypeStruct((lat // T, features), f32),
        ),
        in_specs=[vmem] * 7,
        out_specs=(vmem, vmem),
        scratch_shapes=scratch,
        compiler_params=pltpu.CompilerParams(
            collective_id=0, has_side_effects=True, vmem_limit_bytes=56 * 1024 * 1024
        ),
        cost_estimate=pl.CostEstimate(flops=flops, bytes_accessed=2 * L * features, transcendentals=0),
    )(frames, gain, transition, smoother_gain, smoother_map, emission, noise_precision[None, :])


def solution(mesh):
    in_specs = (P("tm", "shard"), P(None, "shard"), P(), P(), P(), P(None, "shard"), P("shard"))
    out_specs = (P("tm", None), P("tm", "shard"))
    return jax.shard_map(
        on_device, mesh=mesh, in_specs=in_specs, out_specs=out_specs, check_vma=False
    )
```

```python
import functools

import jax
import jax.numpy as jnp
from jax import lax
from jax.experimental import pallas as pl
from jax.experimental.pallas import tpu as pltpu
from jax.sharding import PartitionSpec as P

MESH = pl.DeviceIdType.MESH
CHUNKS = 8


def bits_of(count):
    return count.bit_length() - 1


def split(value):
    high = value.astype(jnp.bfloat16)
    low = (value - high.astype(jnp.float32)).astype(jnp.bfloat16)
    return high, low


def dot(a, b):
    return jnp.dot(a, b, preferred_element_type=jnp.float32)


def dot3(value, right_high, right_low):
    high, low = split(value)
    return dot(high, right_high) + (dot(low, right_high) + dot(high, right_low))


def row_ids(count):
    return lax.broadcasted_iota(jnp.int32, (count, 1), 0)


def kernel(
    T, S,
    frames_in, gain_in, transition, smoother_gain, smoother_map, emission_in, noise,
    smoothed_out, gradient_out,
    frames, gain, emission, part, landed, state, carry_buf, power, fh, fl, gh, gl, ends_f, ends_s, low, low_t, acc, *rest,
):
    stages = bits_of(T)
    inbox = rest[:stages]
    rs_send, rs_recv, ag_send, ag_recv, ef_send, ef_recv, es_send, es_recv, gr_send, gr_recv, block_sem, whole_sem = rest[stages:]
    L, features = frames_in.shape
    lat = gain_in.shape[0]
    rows = L // S
    levels = bits_of(L)
    mt, ms = lax.axis_index("tm"), lax.axis_index("shard")

    barrier = pltpu.get_barrier_semaphore()

    def greet_s(k, c):
        pl.semaphore_signal(barrier, inc=1, device_id=(mt, lax.rem(ms + k, S)), device_id_type=MESH)
        return c

    def greet_t(k, c):
        pl.semaphore_signal(barrier, inc=1, device_id=(lax.rem(mt + k, T), ms), device_id_type=MESH)
        return c

    def block_copy(k):
        there = pl.ds(pl.multiple_of(lax.rem(ms + k, S) * rows, rows), rows)
        return pltpu.make_async_copy(frames_in.at[there], frames.at[there], block_sem.at[k])

    gain_copy = pltpu.make_async_copy(gain_in, gain, whole_sem.at[0])
    emission_copy = pltpu.make_async_copy(emission_in, emission, whole_sem.at[1])
    gain_copy.start()
    for k in list(range(1, S)) + [0]:
        block_copy(k).start()
    emission_copy.start()

    lax.fori_loop(1, S, greet_s, 0)
    lax.fori_loop(1, T, greet_t, 0)

    def scatter_copy(k):
        return pltpu.make_async_remote_copy(
            src_ref=part.at[k], dst_ref=landed.at[k], send_sem=rs_send.at[k], recv_sem=rs_recv.at[k],
            device_id=(mt, lax.rem(ms + k, S)), device_id_type=MESH)

    def partial_drive(k):
        block_copy(k).wait()
        owner = lax.rem(ms + k, S)
        block = frames[pl.ds(pl.multiple_of(owner * rows, rows), rows), :]
        part[k] = lax.dot_general(block, gain[...], (((1,), (1,)), ((), ())), preferred_element_type=jnp.float32)

    def drive_step(k, c):
        partial_drive(k)

        @pl.when(k == 1)
        def _():
            pl.semaphore_wait(barrier, S - 1 + T - 1)

        scatter_copy(k).start()
        return c

    gain_copy.wait()
    lax.fori_loop(1, S, drive_step, 0)
    partial_drive(0)

    power[0] = transition[...].T
    power[1] = smoother_gain[...].T
    fh[0], fl[0] = split(power[0])
    gh[0], gl[0] = split(power[1])

    def square(k, c):
        for i, (h, l) in enumerate(((fh, fl), (gh, gl))):
            value = jnp.dot(power[i], power[i], precision=lax.Precision.HIGHEST, preferred_element_type=jnp.float32)
            power[i] = value
            h[k + 1], l[k + 1] = split(value)
        return c

    early = (levels + stages - 1) // 2
    lax.fori_loop(0, early, square, 0)

    total = part[0]
    for k in range(1, S):
        scatter_copy(k).wait_recv()
        total = total + landed[k]
    mine = pl.ds(pl.multiple_of(ms * rows, rows), rows)
    state[mine, :] = total

    def gather_copy(k):
        return pltpu.make_async_remote_copy(
            src_ref=state.at[mine], dst_ref=state.at[mine], send_sem=ag_send.at[k], recv_sem=ag_recv.at[k],
            device_id=(mt, lax.rem(ms + k, S)), device_id_type=MESH)

    def gather_wait(k):
        source = lax.rem(ms + S - k, S)
        there = state.at[pl.ds(pl.multiple_of(source * rows, rows), rows)]
        pltpu.make_async_remote_copy(
            src_ref=there, dst_ref=there, send_sem=ag_send.at[k], recv_sem=ag_recv.at[k],
            device_id=(mt, lax.rem(ms + k, S)), device_id_type=MESH).wait_recv()

    for k in range(1, S):
        gather_copy(k).start()
    lax.fori_loop(early, levels + stages - 1, square, 0)
    map_h, map_l = split(smoother_map[...].T)
    for k in range(1, S):
        gather_wait(k)
    for k in range(1, S):
        gather_copy(k).wait_send()
        scatter_copy(k).wait_send()

    ids = row_ids(L)

    def local_scan(h, l, backward):
        for level in range(levels):
            d = 1 << level
            if d < 8:
                y = dot3(state[...], h[level], l[level])
                if backward:
                    moved = jnp.where(ids < L - d, pltpu.roll(y, L - d, 0), 0.0)
                else:
                    moved = jnp.where(ids >= d, pltpu.roll(y, d, 0), 0.0)
                state[...] = state[...] + moved
            elif backward:
                y = dot3(state[d:, :], h[level], l[level])
                state[: L - d, :] = state[: L - d, :] + y
            else:
                y = dot3(state[: L - d, :], h[level], l[level])
                state[d:, :] = state[d:, :] + y

    def exchange(ends, edge, send, recv):
        ends[mt] = jnp.broadcast_to(edge, (8, lat))

        def copy(k):
            return pltpu.make_async_remote_copy(
                src_ref=ends.at[mt], dst_ref=ends.at[mt], send_sem=send.at[k], recv_sem=recv.at[k],
                device_id=(lax.rem(mt + k, T), ms), device_id_type=MESH)

        def arrive(k):
            source = lax.rem(mt + T - k, T)
            pltpu.make_async_remote_copy(
                src_ref=ends.at[source], dst_ref=ends.at[source], send_sem=send.at[k], recv_sem=recv.at[k],
                device_id=(lax.rem(mt + k, T), ms), device_id_type=MESH).wait_recv()

        for k in range(1, T):
            copy(k).start()
        for k in range(1, T):
            arrive(k)
        for k in range(1, T):
            copy(k).wait_send()
        value = jnp.concatenate([ends[t, 0:1, :] for t in range(T)], axis=0)
        return value

    def arriving(value, h, l, backward):
        small = row_ids(T)
        for level in range(stages):
            d = 1 << level
            y = dot3(value, h[levels + level], l[levels + level])
            if backward:
                y = jnp.where(small < T - d, pltpu.roll(y, T - d, 0), 0.0)
            else:
                y = jnp.where(small >= d, pltpu.roll(y, d, 0), 0.0)
            value = value + y
        pick = mt + 1 if backward else mt - 1
        return jnp.sum(jnp.where(small == pick, value, 0.0), axis=0, keepdims=True)

    def add_carry(carry, h, l, backward):
        small = row_ids(8)
        exponent = 7 - small if backward else small
        value = dot3(jnp.broadcast_to(carry, (8, lat)), h[0], l[0])
        for level in range(3):
            moved = dot3(value, h[level], l[level])
            value = jnp.where((exponent >> level) & 1 == 1, moved, value)
        if backward:
            carry_buf[L - 8 :, :] = value
        else:
            carry_buf[:8, :] = value
        for level in range(3, levels):
            d = 1 << level
            if backward:
                carry_buf[L - 2 * d : L - d, :] = dot3(carry_buf[L - d :, :], h[level], l[level])
            else:
                carry_buf[d : 2 * d, :] = dot3(carry_buf[:d, :], h[level], l[level])
        state[...] = state[...] + carry_buf[...]

    local_scan(fh, fl, False)
    ends = exchange(ends_f, state[L - 1 :, :], ef_send, ef_recv)
    add_carry(arriving(ends, fh, fl, False), fh, fl, False)

    filtered = state[...]
    own = dot3(filtered, map_h, map_l)
    final_row = (ids == L - 1) & (mt == T - 1)
    state[...] = jnp.where(final_row, filtered, own)

    local_scan(gh, gl, True)
    starts = exchange(ends_s, state[:1, :], es_send, es_recv)
    add_carry(arriving(starts, gh, gl, True), gh, gl, True)

    smoothed = state[...]
    smoothed_out[...] = smoothed
    low[...] = smoothed.astype(jnp.bfloat16)
    low_t[...] = smoothed.T.astype(jnp.bfloat16)

    emission_copy.wait()
    width = features // CHUNKS
    share = lat // T

    def order(c):
        places = list(range(stages))
        return places if c % 2 == 0 else places[:1] + places[:0:-1]

    def bit(place):
        return lax.rem(lax.div(mt, 1 << place), 2)

    def offset(c, stage):
        where = 0
        for earlier in range(stage):
            where = where + bit(order(c)[earlier]) * (T >> (earlier + 1))
        return where

    def halving_copy(c, stage):
        place = order(c)[stage]
        b = bit(place)
        half = T >> (stage + 1)
        partner = mt + (1 - 2 * b) * (1 << place)
        return pltpu.make_async_remote_copy(
            src_ref=acc.at[c, pl.ds(offset(c, stage) + (1 - b) * half, half)],
            dst_ref=inbox[stage].at[c],
            send_sem=gr_send.at[stage, c], recv_sem=gr_recv.at[stage, c],
            device_id=(partner, ms), device_id_type=MESH)

    def compute(c):
        columns = slice(c * width, (c + 1) * width)
        predicted = dot(low[...], emission[:, columns])
        weighted = (noise[:, columns] * (frames[:, columns].astype(jnp.float32) - predicted)).astype(jnp.bfloat16)
        product = dot(low_t[...], weighted)
        for owner in range(T):
            where = 0
            for stage, place in enumerate(order(c)):
                where += (owner >> place & 1) * (T >> (stage + 1))
            acc[c, where] = product[owner * share : (owner + 1) * share, :]

    def take(c, stage):
        halving_copy(c, stage).wait_recv()
        half = T >> (stage + 1)
        keep = pl.ds(offset(c, stage + 1), half)
        acc[c, keep] = acc[c, keep] + inbox[stage][c]

    for step in range(CHUNKS + stages):
        if step < CHUNKS:
            compute(step)
            halving_copy(step, 0).start()
        for stage in range(stages):
            c = step - 1 - stage
            if 0 <= c < CHUNKS:
                take(c, stage)
                if stage + 1 < stages:
                    halving_copy(c, stage + 1).start()
                else:
                    gradient_out[:, c * width : (c + 1) * width] = acc[c, offset(c, stages)] / (L * T)
    for c in range(CHUNKS):
        for stage in range(stages):
            halving_copy(c, stage).wait_send()


def on_device(frames, gain, transition, smoother_gain, smoother_map, emission, noise_precision):
    T, S = lax.axis_size("tm"), lax.axis_size("shard")
    L, features = frames.shape
    lat = gain.shape[0]
    rows = L // S
    stages = bits_of(T)
    levels = bits_of(L) + stages
    width = features // CHUNKS
    f32, b16 = jnp.float32, jnp.bfloat16
    dma = pltpu.SemaphoreType.DMA
    scratch = [
        pltpu.VMEM((L, features), b16),
        pltpu.VMEM((lat, features), b16),
        pltpu.VMEM((lat, features), b16),
        pltpu.VMEM((S, rows, lat), f32),
        pltpu.VMEM((S, rows, lat), f32),
        pltpu.VMEM((L, lat), f32),
        pltpu.VMEM((L, lat), f32),
        pltpu.VMEM((2, lat, lat), f32),
        pltpu.VMEM((levels, lat, lat), b16),
        pltpu.VMEM((levels, lat, lat), b16),
        pltpu.VMEM((levels, lat, lat), b16),
        pltpu.VMEM((levels, lat, lat), b16),
        pltpu.VMEM((T, 8, lat), f32),
        pltpu.VMEM((T, 8, lat), f32),
        pltpu.VMEM((L, lat), b16),
        pltpu.VMEM((lat, L), b16),
        pltpu.VMEM((CHUNKS, T, lat // T, width), f32),
    ]
    scratch += [pltpu.VMEM((CHUNKS, T >> (s + 1), lat // T, width), f32) for s in range(stages)]
    scratch += [dma((S,))] * 4 + [dma((T,))] * 4 + [dma((stages, CHUNKS))] * 2 + [dma((S,)), dma((2,))]
    vmem = pl.BlockSpec(memory_space=pltpu.VMEM)
    hbm = pl.BlockSpec(memory_space=pl.ANY)
    flops = 6 * L * features * lat
    return pl.pallas_call(
        functools.partial(kernel, T, S),
        out_shape=(
            jax.ShapeDtypeStruct((L, lat), f32),
            jax.ShapeDtypeStruct((lat // T, features), f32),
        ),
        in_specs=[hbm, hbm, vmem, vmem, vmem, hbm, vmem],
        out_specs=(vmem, vmem),
        scratch_shapes=scratch,
        compiler_params=pltpu.CompilerParams(
            collective_id=0, has_side_effects=True, vmem_limit_bytes=56 * 1024 * 1024
        ),
        cost_estimate=pl.CostEstimate(flops=flops, bytes_accessed=2 * L * features, transcendentals=0),
    )(frames, gain, transition, smoother_gain, smoother_map, emission, noise_precision[None, :])


def solution(mesh):
    in_specs = (P("tm", "shard"), P(None, "shard"), P(), P(), P(), P(None, "shard"), P("shard"))
    out_specs = (P("tm", None), P("tm", "shard"))
    return jax.shard_map(
        on_device, mesh=mesh, in_specs=in_specs, out_specs=out_specs, check_vma=False
    )
```

```python
import functools

import jax
import jax.numpy as jnp
from jax import lax
from jax.experimental import pallas as pl
from jax.experimental.pallas import tpu as pltpu
from jax.sharding import PartitionSpec as P

MESH = pl.DeviceIdType.MESH
CHUNKS = 4


def bits_of(count):
    return count.bit_length() - 1


def split(value):
    high = value.astype(jnp.bfloat16)
    low = (value - high.astype(jnp.float32)).astype(jnp.bfloat16)
    return high, low


def dot(a, b):
    return jnp.dot(a, b, preferred_element_type=jnp.float32)


def dot3(value, right_high, right_low):
    high, low = split(value)
    return dot(high, right_high) + (dot(low, right_high) + dot(high, right_low))


def row_ids(count):
    return lax.broadcasted_iota(jnp.int32, (count, 1), 0)


def kernel(
    T, S,
    frames_in, gain_in, transition, smoother_gain, smoother_map, emission_in, noise,
    smoothed_out, gradient_out,
    frames, gain, emission, part, landed, state, carry_buf, power, fh, fl, gh, gl, ends_f, ends_s, low, low_t, acc, *rest,
):
    stages = bits_of(T)
    inbox = rest[:stages]
    rs_send, rs_recv, ag_send, ag_recv, ef_send, ef_recv, es_send, es_recv, gr_send, gr_recv, block_sem, whole_sem = rest[stages:]
    L, features = frames_in.shape
    lat = gain_in.shape[0]
    rows = L // S
    levels = bits_of(L)
    mt, ms = lax.axis_index("tm"), lax.axis_index("shard")

    barrier = pltpu.get_barrier_semaphore()

    def greet_s(k, c):
        pl.semaphore_signal(barrier, inc=1, device_id=(mt, lax.rem(ms + k, S)), device_id_type=MESH)
        return c

    def greet_t(k, c):
        pl.semaphore_signal(barrier, inc=1, device_id=(lax.rem(mt + k, T), ms), device_id_type=MESH)
        return c

    def block_copy(k):
        there = pl.ds(pl.multiple_of(lax.rem(ms + k, S) * rows, rows), rows)
        return pltpu.make_async_copy(frames_in.at[there], frames.at[there], block_sem.at[k])

    gain_copy = pltpu.make_async_copy(gain_in, gain, whole_sem.at[0])
    emission_copy = pltpu.make_async_copy(emission_in, emission, whole_sem.at[1])
    gain_copy.start()
    for k in list(range(1, S)) + [0]:
        block_copy(k).start()
    emission_copy.start()

    lax.fori_loop(1, S, greet_s, 0)
    lax.fori_loop(1, T, greet_t, 0)

    def scatter_copy(k):
        return pltpu.make_async_remote_copy(
            src_ref=part.at[k], dst_ref=landed.at[k], send_sem=rs_send.at[k], recv_sem=rs_recv.at[k],
            device_id=(mt, lax.rem(ms + k, S)), device_id_type=MESH)

    def partial_drive(k):
        block_copy(k).wait()
        owner = lax.rem(ms + k, S)
        block = frames[pl.ds(pl.multiple_of(owner * rows, rows), rows), :]
        part[k] = lax.dot_general(block, gain[...], (((1,), (1,)), ((), ())), preferred_element_type=jnp.float32)

    def drive_step(k, c):
        partial_drive(k)

        @pl.when(k == 1)
        def _():
            pl.semaphore_wait(barrier, S - 1 + T - 1)

        scatter_copy(k).start()
        return c

    gain_copy.wait()
    lax.fori_loop(1, S, drive_step, 0)
    partial_drive(0)

    power[0] = transition[...].T
    power[1] = smoother_gain[...].T
    fh[0], fl[0] = split(power[0])
    gh[0], gl[0] = split(power[1])

    def square(k, c):
        for i, (h, l) in enumerate(((fh, fl), (gh, gl))):
            value = jnp.dot(power[i], power[i], precision=lax.Precision.HIGHEST, preferred_element_type=jnp.float32)
            power[i] = value
            h[k + 1], l[k + 1] = split(value)
        return c

    early = (levels + stages - 1) // 2
    lax.fori_loop(0, early, square, 0)

    total = part[0]
    for k in range(1, S):
        scatter_copy(k).wait_recv()
        total = total + landed[k]
    mine = pl.ds(pl.multiple_of(ms * rows, rows), rows)
    state[mine, :] = total

    def gather_copy(k):
        return pltpu.make_async_remote_copy(
            src_ref=state.at[mine], dst_ref=state.at[mine], send_sem=ag_send.at[k], recv_sem=ag_recv.at[k],
            device_id=(mt, lax.rem(ms + k, S)), device_id_type=MESH)

    def gather_wait(k):
        source = lax.rem(ms + S - k, S)
        there = state.at[pl.ds(pl.multiple_of(source * rows, rows), rows)]
        pltpu.make_async_remote_copy(
            src_ref=there, dst_ref=there, send_sem=ag_send.at[k], recv_sem=ag_recv.at[k],
            device_id=(mt, lax.rem(ms + k, S)), device_id_type=MESH).wait_recv()

    for k in range(1, S):
        gather_copy(k).start()
    lax.fori_loop(early, levels + stages - 1, square, 0)
    map_h, map_l = split(smoother_map[...].T)
    for k in range(1, S):
        gather_wait(k)
    for k in range(1, S):
        gather_copy(k).wait_send()
        scatter_copy(k).wait_send()

    ids = row_ids(L)

    def local_scan(h, l, backward):
        for level in range(levels):
            d = 1 << level
            if d < 8:
                y = dot3(state[...], h[level], l[level])
                if backward:
                    moved = jnp.where(ids < L - d, pltpu.roll(y, L - d, 0), 0.0)
                else:
                    moved = jnp.where(ids >= d, pltpu.roll(y, d, 0), 0.0)
                state[...] = state[...] + moved
            elif backward:
                y = dot3(state[d:, :], h[level], l[level])
                state[: L - d, :] = state[: L - d, :] + y
            else:
                y = dot3(state[: L - d, :], h[level], l[level])
                state[d:, :] = state[d:, :] + y

    def exchange(ends, edge, send, recv):
        ends[mt] = jnp.broadcast_to(edge, (8, lat))

        def copy(k):
            return pltpu.make_async_remote_copy(
                src_ref=ends.at[mt], dst_ref=ends.at[mt], send_sem=send.at[k], recv_sem=recv.at[k],
                device_id=(lax.rem(mt + k, T), ms), device_id_type=MESH)

        def arrive(k):
            source = lax.rem(mt + T - k, T)
            pltpu.make_async_remote_copy(
                src_ref=ends.at[source], dst_ref=ends.at[source], send_sem=send.at[k], recv_sem=recv.at[k],
                device_id=(lax.rem(mt + k, T), ms), device_id_type=MESH).wait_recv()

        for k in range(1, T):
            copy(k).start()
        for k in range(1, T):
            arrive(k)
        for k in range(1, T):
            copy(k).wait_send()
        value = jnp.concatenate([ends[t, 0:1, :] for t in range(T)], axis=0)
        return value

    def arriving(value, h, l, backward):
        small = row_ids(T)
        for level in range(stages):
            d = 1 << level
            y = dot3(value, h[levels + level], l[levels + level])
            if backward:
                y = jnp.where(small < T - d, pltpu.roll(y, T - d, 0), 0.0)
            else:
                y = jnp.where(small >= d, pltpu.roll(y, d, 0), 0.0)
            value = value + y
        pick = mt + 1 if backward else mt - 1
        return jnp.sum(jnp.where(small == pick, value, 0.0), axis=0, keepdims=True)

    def add_carry(carry, h, l, backward):
        small = row_ids(8)
        exponent = 7 - small if backward else small
        value = dot3(jnp.broadcast_to(carry, (8, lat)), h[0], l[0])
        for level in range(3):
            moved = dot3(value, h[level], l[level])
            value = jnp.where((exponent >> level) & 1 == 1, moved, value)
        if backward:
            carry_buf[L - 8 :, :] = value
        else:
            carry_buf[:8, :] = value
        for level in range(3, levels):
            d = 1 << level
            if backward:
                carry_buf[L - 2 * d : L - d, :] = dot3(carry_buf[L - d :, :], h[level], l[level])
            else:
                carry_buf[d : 2 * d, :] = dot3(carry_buf[:d, :], h[level], l[level])
        state[...] = state[...] + carry_buf[...]

    local_scan(fh, fl, False)
    ends = exchange(ends_f, state[L - 1 :, :], ef_send, ef_recv)
    add_carry(arriving(ends, fh, fl, False), fh, fl, False)

    filtered = state[...]
    own = dot3(filtered, map_h, map_l)
    final_row = (ids == L - 1) & (mt == T - 1)
    state[...] = jnp.where(final_row, filtered, own)

    local_scan(gh, gl, True)
    starts = exchange(ends_s, state[:1, :], es_send, es_recv)
    add_carry(arriving(starts, gh, gl, True), gh, gl, True)

    smoothed = state[...]
    smoothed_out[...] = smoothed
    low[...] = smoothed.astype(jnp.bfloat16)
    low_t[...] = smoothed.T.astype(jnp.bfloat16)

    emission_copy.wait()
    width = features // CHUNKS
    share = lat // T

    def order(c):
        places = list(range(stages))
        return places if c % 2 == 0 else places[:1] + places[:0:-1]

    def bit(place):
        return lax.rem(lax.div(mt, 1 << place), 2)

    def offset(c, stage):
        where = 0
        for earlier in range(stage):
            where = where + bit(order(c)[earlier]) * (T >> (earlier + 1))
        return where

    def halving_copy(c, stage):
        place = order(c)[stage]
        b = bit(place)
        half = T >> (stage + 1)
        partner = mt + (1 - 2 * b) * (1 << place)
        return pltpu.make_async_remote_copy(
            src_ref=acc.at[c, pl.ds(offset(c, stage) + (1 - b) * half, half)],
            dst_ref=inbox[stage].at[c],
            send_sem=gr_send.at[stage, c], recv_sem=gr_recv.at[stage, c],
            device_id=(partner, ms), device_id_type=MESH)

    def compute(c):
        columns = slice(c * width, (c + 1) * width)
        predicted = dot(low[...], emission[:, columns])
        weighted = (noise[:, columns] * (frames[:, columns].astype(jnp.float32) - predicted)).astype(jnp.bfloat16)
        product = dot(low_t[...], weighted)
        for owner in range(T):
            where = 0
            for stage, place in enumerate(order(c)):
                where += (owner >> place & 1) * (T >> (stage + 1))
            acc[c, where] = product[owner * share : (owner + 1) * share, :]

    def take(c, stage):
        halving_copy(c, stage).wait_recv()
        half = T >> (stage + 1)
        keep = pl.ds(offset(c, stage + 1), half)
        acc[c, keep] = acc[c, keep] + inbox[stage][c]

    for step in range(CHUNKS + stages):
        if step < CHUNKS:
            compute(step)
            halving_copy(step, 0).start()
        for stage in range(stages):
            c = step - 1 - stage
            if 0 <= c < CHUNKS:
                take(c, stage)
                if stage + 1 < stages:
                    halving_copy(c, stage + 1).start()
                else:
                    gradient_out[:, c * width : (c + 1) * width] = acc[c, offset(c, stages)]
    for c in range(CHUNKS):
        for stage in range(stages):
            halving_copy(c, stage).wait_send()


def on_device(frames, gain, transition, smoother_gain, smoother_map, emission, noise_precision):
    T, S = lax.axis_size("tm"), lax.axis_size("shard")
    L, features = frames.shape
    lat = gain.shape[0]
    rows = L // S
    stages = bits_of(T)
    levels = bits_of(L) + stages
    width = features // CHUNKS
    f32, b16 = jnp.float32, jnp.bfloat16
    dma = pltpu.SemaphoreType.DMA
    scratch = [
        pltpu.VMEM((L, features), b16),
        pltpu.VMEM((lat, features), b16),
        pltpu.VMEM((lat, features), b16),
        pltpu.VMEM((S, rows, lat), f32),
        pltpu.VMEM((S, rows, lat), f32),
        pltpu.VMEM((L, lat), f32),
        pltpu.VMEM((L, lat), f32),
        pltpu.VMEM((2, lat, lat), f32),
        pltpu.VMEM((levels, lat, lat), b16),
        pltpu.VMEM((levels, lat, lat), b16),
        pltpu.VMEM((levels, lat, lat), b16),
        pltpu.VMEM((levels, lat, lat), b16),
        pltpu.VMEM((T, 8, lat), f32),
        pltpu.VMEM((T, 8, lat), f32),
        pltpu.VMEM((L, lat), b16),
        pltpu.VMEM((lat, L), b16),
        pltpu.VMEM((CHUNKS, T, lat // T, width), f32),
    ]
    scratch += [pltpu.VMEM((CHUNKS, T >> (s + 1), lat // T, width), f32) for s in range(stages)]
    scratch += [dma((S,))] * 4 + [dma((T,))] * 4 + [dma((stages, CHUNKS))] * 2 + [dma((S,)), dma((2,))]
    vmem = pl.BlockSpec(memory_space=pltpu.VMEM)
    hbm = pl.BlockSpec(memory_space=pl.ANY)
    flops = 6 * L * features * lat
    smoothed, total = pl.pallas_call(
        functools.partial(kernel, T, S),
        out_shape=(
            jax.ShapeDtypeStruct((L, lat), f32),
            jax.ShapeDtypeStruct((lat // T, features), f32),
        ),
        in_specs=[hbm, hbm, vmem, vmem, vmem, hbm, vmem],
        out_specs=(vmem, vmem),
        scratch_shapes=scratch,
        compiler_params=pltpu.CompilerParams(
            collective_id=0, has_side_effects=True, vmem_limit_bytes=56 * 1024 * 1024
        ),
        cost_estimate=pl.CostEstimate(flops=flops, bytes_accessed=2 * L * features, transcendentals=0),
    )(frames, gain, transition, smoother_gain, smoother_map, emission, noise_precision[None, :])
    return smoothed, total / (L * T)


def solution(mesh):
    in_specs = (P("tm", "shard"), P(None, "shard"), P(), P(), P(), P(None, "shard"), P("shard"))
    out_specs = (P("tm", None), P("tm", "shard"))
    return jax.shard_map(
        on_device, mesh=mesh, in_specs=in_specs, out_specs=out_specs, check_vma=False
    )
```
